32 devices in a mesh: dp: 8 (over z, core), fsdp: 4 (over y, x).
Axes of the slice: x: 2, y: 2, z: 4, core: 2. Of those that a mesh axis runs over, the one named last changes fastest.
Arguments:
- inputs: bfloat16 [8, 1152, 2048], P('dp', 'fsdp'), may hold values from -6 to 6
- modality: int32 [8, 1152], P('dp', 'fsdp'), may hold values from 0 to 2, as said below
- gain: bfloat16 [2048], P(('dp', 'fsdp')), may hold values from 0.5 to 1.5
- in_weight: bfloat16 [3, 2048, 8192], P(None, None, ('dp', 'fsdp')), may hold values from -0.125 to 0.125
- conv_weight: bfloat16 [4, 4096], P(None, ('dp', 'fsdp')), may hold values from -0.5 to 0.5
- conv_bias: bfloat16 [4096], P(('dp', 'fsdp')), may hold values from -0.5 to 0.5
- x_weight: bfloat16 [3, 4096, 160], P(None, ('dp', 'fsdp')), may hold values from -0.09375 to 0.09375
- dt_weight: bfloat16 [3, 128, 4096], P(None, None, ('dp', 'fsdp')), may hold values from -0.5 to 0.5
- dt_bias: bfloat16 [3, 4096], P(None, ('dp', 'fsdp')), may hold values from -5.5 to -3.5
- log_rate: bfloat16 [16, 4096], P(None, ('dp', 'fsdp')), may hold values from -3 to 1.59375
- skip_gain: bfloat16 [4096], P(('dp', 'fsdp')), may hold values from 0.5 to 1.5
- out_weight: bfloat16 [3, 4096, 2048], P(None, ('dp', 'fsdp')), may hold values from -0.25 to 0.25
- out_grad: bfloat16 [8, 1152, 2048], P('dp', 'fsdp'), may hold values from -6 to 6
Outputs:
- output: bfloat16 [8, 1152, 2048], P('dp', 'fsdp')
- input_grad: float32 [8, 1152, 2048], P('dp', 'fsdp')
- gain_grad: float32 [2048], P(('dp', 'fsdp'))
- in_weight_grad: float32 [3, 2048, 8192], P(None, None, ('dp', 'fsdp'))
- conv_weight_grad: float32 [4, 4096], P(None, ('dp', 'fsdp'))
- conv_bias_grad: float32 [4096], P(('dp', 'fsdp'))
- x_weight_grad: float32 [3, 4096, 160], P(None, ('dp', 'fsdp'))
- dt_weight_grad: float32 [3, 128, 4096], P(None, None, ('dp', 'fsdp'))
- dt_bias_grad: float32 [3, 4096], P(None, ('dp', 'fsdp'))
- log_rate_grad: float32 [16, 4096], P(None, ('dp', 'fsdp'))
- skip_gain_grad: float32 [4096], P(('dp', 'fsdp'))
- out_weight_grad: float32 [3, 4096, 2048], P(None, ('dp', 'fsdp'))
The draws below stay inside these ranges and needn't reach their ends.
Inputs may be any that keep to these rules, and one draw needn't show every extreme that they name: The modality of each token, one of 3.
All inputs are finite; a program needn't handle non-finite values.
Results may differ from the reference program's by a relative error of at most 0.0081.
The reference program's roundings to bfloat16 on the way (of `normed`, `mixed` and `gated`) count: a program that leaves them out, or rounds other values in their place, can miss the bound.
Values may be sent and summed in bfloat16 or wider, within the bound.
No kernel may reach another device: no remote copies, remote signals or barrier semaphores. Data moves between devices by JAX's collectives and lax.ppermute only.
A program may use at most 640 MiB of HBM per device.

```python
import math
import jax
import jax.numpy as jnp
from jax import lax

D = 2048
E = 4096
NS = 16
KC = 4
R = 128
MODES = 3
SEQ_LEN = 1152
BATCH = 8


def draw_modality(key, part):
    key = jax.random.fold_in(key, 11)
    heavy_key, pick_key, other_key = jax.random.split(key, 3)
    heavy = jax.random.randint(heavy_key, (BATCH, 1), 0, MODES)
    picked = jax.random.randint(pick_key, (BATCH, SEQ_LEN), 0, 10)
    others = jax.random.randint(other_key, (BATCH, SEQ_LEN), 1, MODES)
    return jnp.where(picked < 7, heavy, (heavy + others) % MODES).astype(jnp.int32)


def shard_levels(key, shape, pieces, low, high):
    loudness, own = 1.0, jax.random.fold_in(key, 6)
    for position, parts in pieces:
        heights = jnp.exp(jax.random.uniform(jax.random.fold_in(own, position), (parts,), jnp.float32, low / len(pieces), high / len(pieces)))
        loudness = loudness * jnp.repeat(heights, shape[position] // parts).reshape([-1 if axis == position else 1 for axis in range(len(shape))])
    return loudness


def noise(rng, extent, deviation, limit, cuts=(), kind=jnp.bfloat16):
    result = deviation * jax.random.normal(rng, extent, jnp.float32)
    if cuts:
        result = result * shard_levels(rng, extent, cuts, -0.22, 0.18)
    return jnp.clip(result, -limit, limit).astype(kind)


def setup_inputs(seed: int = 0) -> dict:
    splits = jax.random.split(jax.random.key(seed), 14)
    return {
        "inputs": noise(splits[0], (BATCH, SEQ_LEN, D), 1.0, 6.0, ((0, 8), (1, 4))),
        "modality": draw_modality(jax.random.fold_in(splits[13], 71), 0),
        "gain": jnp.clip(1.0 + 0.1 * jax.random.normal(splits[2], (D,), jnp.float32), 0.5, 1.5).astype(jnp.bfloat16),
        "in_weight": noise(splits[3], (MODES, D, 2 * E), D ** -0.5, 0.125, ((2, 32),)),
        "conv_weight": jnp.clip(jax.random.uniform(splits[4], (KC, E), jnp.float32, -0.5, 0.5) * shard_levels(splits[4], (KC, E), ((1, 32),), -0.4, 0.0), -0.5, 0.5).astype(jnp.bfloat16),
        "conv_bias": jnp.clip(jax.random.uniform(splits[5], (E,), jnp.float32, -0.5, 0.5) * shard_levels(splits[5], (E,), ((0, 32),), -0.4, 0.0), -0.5, 0.5).astype(jnp.bfloat16),
        "x_weight": noise(splits[6], (MODES, E, R + 2 * NS), E ** -0.5, 0.09375, ((1, 32),)),
        "dt_weight": noise(splits[7], (MODES, R, E), R ** -0.5, 0.5, ((2, 32),)),
        "dt_bias": jnp.clip(-5.5 + 2.0 * jax.random.uniform(splits[8], (MODES, E), jnp.float32) ** shard_levels(splits[8], (MODES, E), ((1, 32),), -0.2, 0.2), -5.5, -3.5).astype(jnp.bfloat16),
        "log_rate": jnp.clip(-3.0 + 4.59375 * jax.random.uniform(splits[9], (NS, E), jnp.float32) ** shard_levels(splits[9], (NS, E), ((1, 32),), -0.2, 0.2), -3.0, 1.59375).astype(jnp.bfloat16),
        "skip_gain": jnp.clip(0.5 + 1.0 * jax.random.uniform(splits[10], (E,), jnp.float32) ** shard_levels(splits[10], (E,), ((0, 32),), -0.2, 0.2), 0.5, 1.5).astype(jnp.bfloat16),
        "out_weight": noise(splits[11], (MODES, E, D), (E // 8) ** -0.5, 0.25, ((1, 32),)),
        "out_grad": noise(splits[12], (BATCH, SEQ_LEN, D), 1.0, 6.0, ((0, 8), (1, 4))),
    }


epsilon = 1e-05
highest = lax.Precision.HIGHEST

@jax.custom_vjp
def low(v):
    return lax.optimization_barrier(v.astype(jnp.bfloat16)).astype(jnp.float32)

@jax.custom_vjp
def low_back(v):
    return v

def low_keep(v):
    return (low(v), None)

def low_pass(kept, grad):
    return (grad,)

def back_keep(v):
    return (v, None)

def back_low(kept, grad):
    return (low(grad),)
low.defvjp(low_keep, low_pass)
low_back.defvjp(back_keep, back_low)

def time_blocks(values):
    seq_count, length, width = values.shape
    block_len = math.gcd(16, length)
    moved = jnp.swapaxes(values, 0, 1)
    return moved.reshape(length // block_len, block_len, seq_count, width)

def from_blocks(values, seq_count):
    count, block_len, _, width = values.shape
    return jnp.swapaxes(values.reshape(count * block_len, seq_count, width), 0, 1)

def advance(state, d_row, u_row, b_row, rate):
    return jnp.exp(d_row[:, None, :] * rate) * state + (d_row * u_row)[:, None, :] * b_row[:, :, None]

def scan_all(delta, u_act, b_in, c_out, rate):
    seq_count = delta.shape[0]
    start = jnp.zeros((seq_count, rate.shape[0], rate.shape[1]), jnp.float32)

    def block_fn(state, block):
        d_blk, u_blk, b_blk, c_blk = block
        rows = []
        for index in range(d_blk.shape[0]):
            state = advance(state, d_blk[index], u_blk[index], b_blk[index], rate)
            rows.append(lax.optimization_barrier(jnp.sum(c_blk[index][:, :, None] * state, axis=1)))
        return (state, jnp.stack(rows))
    _, outs = lax.scan(jax.checkpoint(block_fn), start, (time_blocks(delta), time_blocks(u_act), time_blocks(b_in), time_blocks(c_out)))
    return from_blocks(outs, seq_count)

def mode_product(left, weight, masks):
    total = masks[..., 0:1] * jnp.dot(left, weight[0], precision=highest)
    for copy_index in range(1, weight.shape[0]):
        total = total + masks[..., copy_index:copy_index + 1] * jnp.dot(left, weight[copy_index], precision=highest)
    return total

def forward(inputs, gain, in_weight, conv_weight, conv_bias, x_weight, dt_weight, dt_bias, log_rate, skip_gain, out_weight, masks):
    mean_sq = lax.optimization_barrier(jnp.mean(inputs * inputs, axis=-1, keepdims=True))
    normed = low(inputs * lax.rsqrt(mean_sq + epsilon) * gain)
    mixed = low_back(low(mode_product(normed, in_weight, masks)))
    width = conv_weight.shape[1]
    u_pre = mixed[..., :width]
    z_gate = mixed[..., width:]
    taps = conv_weight.shape[0]
    length = u_pre.shape[1]
    padded = jnp.pad(u_pre, ((0, 0), (taps - 1, 0), (0, 0)))
    conv = conv_bias
    for tap in range(taps):
        conv = conv + conv_weight[tap] * padded[:, tap:tap + length, :]
    u_act = jax.nn.silu(conv)
    proj = low_back(mode_product(low(u_act), x_weight, masks))
    rank = dt_weight.shape[1]
    states = log_rate.shape[0]
    dt_rank = low(proj[..., :rank])
    b_in = proj[..., rank:rank + states]
    c_out = proj[..., rank + states:]
    raw = low_back(mode_product(dt_rank, dt_weight, masks) + jnp.dot(masks, dt_bias, precision=highest))
    delta = jax.nn.softplus(raw)
    rate = -jnp.exp(log_rate)
    y_scan = scan_all(delta, u_act, b_in, c_out, rate)
    gated = low((y_scan + skip_gain * u_act) * jax.nn.silu(z_gate))
    return inputs + mode_product(gated, out_weight, masks)

def reference(inputs, modality, gain, in_weight, conv_weight, conv_bias, x_weight, dt_weight, dt_bias, log_rate, skip_gain, out_weight, out_grad):
    masks = (modality[..., None] == jnp.arange(in_weight.shape[0], dtype=jnp.int32)).astype(jnp.float32)

    def apply_block(inputs_f, gain_f, in_f, conv_f, cbias_f, select_f, step_f, sbias_f, rate_f, skip_f, outer_f):
        return forward(inputs_f, gain_f, in_f, conv_f, cbias_f, select_f, step_f, sbias_f, rate_f, skip_f, outer_f, masks)
    output, pull = jax.vjp(apply_block, inputs.astype(jnp.float32), gain.astype(jnp.float32), in_weight.astype(jnp.float32), conv_weight.astype(jnp.float32), conv_bias.astype(jnp.float32), x_weight.astype(jnp.float32), dt_weight.astype(jnp.float32), dt_bias.astype(jnp.float32), log_rate.astype(jnp.float32), skip_gain.astype(jnp.float32), out_weight.astype(jnp.float32))
    input_grad, gain_grad, in_grad, conv_grad, cbias_grad, select_grad, step_grad, sbias_grad, rate_grad, skip_grad, outer_grad = pull(out_grad.astype(jnp.float32))
    return (output.astype(jnp.bfloat16), input_grad, gain_grad, in_grad, conv_grad, cbias_grad, select_grad, step_grad, sbias_grad, rate_grad, skip_grad, outer_grad)
```

```python
import functools
import math

import jax
import jax.numpy as jnp
from jax import lax
from jax.experimental import pallas as pl
from jax.experimental.pallas import tpu as pltpu
from jax.sharding import PartitionSpec as P

epsilon = 1e-05
LANES = 128
SUB = 8


def spread_maps(parts_ref, ones_ref, spread, first, last):
    chunk = spread.shape[0]
    for n in range(first, last, 2):
        both = jnp.dot(
            parts_ref[...],
            ones_ref[:, n * LANES : (n + 2) * LANES],
            preferred_element_type=jnp.float32,
        )
        spread[:, n] = both[:, :LANES].reshape(chunk, SUB, LANES)
        spread[:, n + 1] = both[:, LANES:].reshape(chunk, SUB, LANES)


def lane_blocks(width):
    return [pl.ds(start, LANES) for start in range(0, width, LANES)]


def state_blocks(states):
    return [(0, states // 2), (states // 2, states)]


def end_kernel(d_ref, u_ref, parts_ref, ones_ref, rate_ref, end_ref, sum_ref, spread):
    @pl.when(pl.program_id(1) == 0)
    def _():
        end_ref[...] = jnp.zeros_like(end_ref)
        sum_ref[...] = jnp.zeros_like(sum_ref)

    chunk, states = d_ref.shape[0], rate_ref.shape[0]
    spread_maps(parts_ref, ones_ref, spread, 0, states)
    for lanes in lane_blocks(d_ref.shape[2]):
        sum_ref[:, lanes] += jnp.sum(d_ref[:, :, lanes], axis=0)
        rate = rate_ref[:, :, lanes]

        def body(t, state):
            d, u = d_ref[t, :, lanes], u_ref[t, :, lanes]
            return jnp.exp2(d[None] * rate) * state + (d * u)[None] * spread[t, :states]

        end_ref[:, :, lanes] = lax.fori_loop(0, chunk, body, end_ref[:, :, lanes], unroll=4)


def ahead_kernel(d_ref, y_ref, parts_ref, ones_ref, rate_ref, out_ref, spread):
    @pl.when(pl.program_id(1) == 0)
    def _():
        out_ref[...] = jnp.zeros_like(out_ref)

    chunk, states = d_ref.shape[0], rate_ref.shape[0]
    spread_maps(parts_ref, ones_ref, spread, states, 2 * states)
    for lanes in lane_blocks(d_ref.shape[2]):
        rate = rate_ref[:, :, lanes]

        def body(k, grad):
            t = chunk - 1 - k
            d, dy = d_ref[t, :, lanes], y_ref[t, :, lanes]
            return jnp.exp2(d[None] * rate) * (grad + dy[None] * spread[t, states:])

        out_ref[:, :, lanes] = lax.fori_loop(0, chunk, body, out_ref[:, :, lanes], unroll=4)


def forward_kernel(
    d_ref, u_ref, parts_ref, ones_ref, rate_ref, start_ref, *refs
):
    y_ref, kept_ref, state_ref, spread = refs[-4:]

    @pl.when(pl.program_id(1) == 0)
    def _():
        state_ref[...] = start_ref[...]

    chunk, states = d_ref.shape[0], rate_ref.shape[0]
    spread_maps(parts_ref, ones_ref, spread, 0, 2 * states)
    kept_ref[0] = state_ref[...]
    for lanes in lane_blocks(d_ref.shape[2]):
        rate = rate_ref[:, :, lanes]

        def body(t, state):
            d, u = d_ref[t, :, lanes], u_ref[t, :, lanes]
            state = jnp.exp2(d[None] * rate) * state + (d * u)[None] * spread[t, :states]
            y_ref[t, :, lanes] = jnp.sum(state * spread[t, states:], axis=0)
            return state

        state_ref[:, :, lanes] = lax.fori_loop(0, chunk, body, state_ref[:, :, lanes], unroll=4)


def backward_kernel(
    d_ref,
    u_ref,
    y_ref,
    parts_ref,
    ones_ref,
    rate_ref,
    kept_ref,
    start_ref,
    *refs,
):
    du_ref, dd_ref, dmaps_ref, drate_ref, grad_ref, spread, held, factors, partial = refs[-9:]

    @pl.when(pl.program_id(1) == 0)
    def _():
        grad_ref[...] = start_ref[...]
        drate_ref[...] = jnp.zeros_like(drate_ref)

    chunk, states = d_ref.shape[0], rate_ref.shape[0]
    natural = math.log(2.0)
    spread_maps(parts_ref, ones_ref, spread, 0, 2 * states)
    for index, lanes in enumerate(lane_blocks(d_ref.shape[2])):
        for low, high in state_blocks(states):
            rate = rate_ref[low:high, :, lanes]
            held[0] = kept_ref[0, low:high, :, lanes]

            def forward(t, state):
                d, u = d_ref[t, :, lanes], u_ref[t, :, lanes]
                factor = jnp.exp2(d[None] * rate)
                state = factor * state + (d * u)[None] * spread[t, low:high]
                factors[t] = factor
                held[t + 1] = state
                return state

            lax.fori_loop(0, chunk, forward, held[0], unroll=4)

            def backward(k, carry):
                t = chunk - 1 - k
                ahead, drate = carry
                d, u, dy = d_ref[t, :, lanes], u_ref[t, :, lanes], y_ref[t, :, lanes]
                grad = spread[t, states + low : states + high] * dy[None] + ahead
                part_b = (d * u)[None] * grad
                part_c = dy[None] * held[t + 1]
                if index == 0:
                    partial[t, low:high] = part_b
                    partial[t, states + low : states + high] = part_c
                else:
                    partial[t, low:high] += part_b
                    partial[t, states + low : states + high] += part_c
                through = jnp.sum(grad * spread[t, low:high], axis=0)
                ahead = factors[t] * grad
                moved = ahead * held[t]
                du, dd = d * through, natural * jnp.sum(moved * rate, axis=0) + u * through
                if low == 0:
                    du_ref[t, :, lanes] = du
                    dd_ref[t, :, lanes] = dd
                else:
                    du_ref[t, :, lanes] += du
                    dd_ref[t, :, lanes] += dd
                return ahead, drate + d[None] * moved

            ahead, drate = lax.fori_loop(
                0,
                chunk,
                backward,
                (grad_ref[low:high, :, lanes], drate_ref[low:high, :, lanes]),
                unroll=4,
            )
            grad_ref[low:high, :, lanes] = ahead
            drate_ref[low:high, :, lanes] = drate

    column = lax.broadcasted_iota(jnp.int32, (SUB, LANES), 1)

    def gather(t, _):
        total = jnp.zeros((SUB, LANES), jnp.float32)
        for n in range(2 * states):
            total = jnp.where(column == n, jnp.sum(partial[t, n], axis=1, keepdims=True), total)
        dmaps_ref[t] = total[:, : 2 * states]
        return 0

    lax.fori_loop(0, chunk, gather, 0, unroll=4)


def scan_call(kernel, delta, states, reverse, ins, outs, scratch, cost, after=()):
    length, count, width = delta.shape
    chunk = math.gcd(16, length)
    steps = length // chunk

    def at(t):
        return steps - 1 - t if reverse else t

    specs = {
        "rows": (
            pl.BlockSpec((chunk, SUB, width), lambda b, t: (at(t), b, 0)),
            (length, count, width),
        ),
        "maps": (
            pl.BlockSpec((chunk, SUB, 2 * states), lambda b, t: (at(t), b, 0)),
            (length, count, 2 * states),
        ),
        "parts": (
            pl.BlockSpec((None, chunk * SUB, 6 * states), lambda b, t: (b, at(t), 0)),
            (count // SUB, length * SUB, 6 * states),
        ),
        "ones": (
            pl.BlockSpec((6 * states, 2 * states * LANES), lambda b, t: (0, 0)),
            (6 * states, 2 * states * LANES),
        ),
        "state": (
            pl.BlockSpec((states, SUB, width), lambda b, t: (0, b, 0)),
            (states, count, width),
        ),
        "rate": (
            pl.BlockSpec((states, SUB, width), lambda b, t: (0, 0, 0)),
            (states, SUB, width),
        ),
        "kept": (
            pl.BlockSpec((1, states, SUB, width), lambda b, t: (at(t), 0, b, 0)),
            (steps, states, count, width),
        ),
        "sum": (pl.BlockSpec((SUB, width), lambda b, t: (b, 0)), (count, width)),
    }
    sizes = {
        "spread": pltpu.VMEM((chunk, 2 * states, SUB, LANES), jnp.float32),
        "held": pltpu.VMEM((chunk + 1, states // 2, SUB, LANES), jnp.float32),
        "factors": pltpu.VMEM((chunk, states // 2, SUB, LANES), jnp.float32),
        "state": pltpu.VMEM((states, SUB, width), jnp.float32),
    }
    return pl.pallas_call(
        kernel,
        grid=(count // SUB, steps),
        in_specs=[specs[name][0] for name, _ in ins]
        + [pl.BlockSpec(memory_space=pl.ANY) for _ in after],
        out_specs=[specs[name][0] for name in outs],
        out_shape=[jax.ShapeDtypeStruct(specs[name][1], jnp.float32) for name in outs],
        scratch_shapes=[sizes[name] for name in scratch],
        compiler_params=pltpu.CompilerParams(vmem_limit_bytes=40 * 1024 * 1024),
        cost_estimate=pl.CostEstimate(
            flops=length * count * width * states * cost * 300,
            bytes_accessed=length * count * width * 4 * (len(ins) + len(outs)),
            transcendentals=length * count * width * states,
        ),
    )(*[value for _, value in ins], *after)


def masked(left, masks):
    return left[:, None, :] * masks.astype(left.dtype)[:, :, None]


def mode_dot(left, weight, masks):
    return lax.dot_general(
        masked(left, masks), weight, (((1, 2), (0, 1)), ((), ())), preferred_element_type=jnp.float32
    )


def mode_dot_back(left, weight, masks):
    return lax.dot_general(
        masked(left, masks), weight, (((1, 2), (0, 2)), ((), ())), preferred_element_type=jnp.float32
    )


def mode_outer(left, right, masks):
    return lax.dot_general(
        masked(left, masks), right, (((0,), (0,)), ((), ())), preferred_element_type=jnp.float32
    )


def exchanged(value, axis, mask):
    count = lax.axis_size(axis)
    return lax.ppermute(value, axis, [(source, source ^ mask) for source in range(count)])


def gathered(value, axis, dimension):
    pieces = [value] + [exchanged(value, axis, m) for m in range(1, lax.axis_size(axis))]
    return jnp.concatenate(pieces, axis=dimension)


def piece_of(pieces, index):
    return lax.dynamic_index_in_dim(pieces, index, axis=0, keepdims=False)


def then(*values):
    return lax.optimization_barrier(values)


def core_sent(pieces, kind):
    core = lax.axis_index("dp") % 2
    pairs = pieces.reshape((pieces.shape[0] // 2, 2) + pieces.shape[1:])
    kept = lax.dynamic_index_in_dim(pairs, core, axis=1, keepdims=False)
    other = lax.dynamic_index_in_dim(pairs, 1 - core, axis=1, keepdims=False)
    return kept, exchanged(other.astype(kind), "dp", 1)


def chips_sent(kept, other, kind):
    place = lax.axis_index("dp") // 2
    both = kept.astype(jnp.float32) + other.astype(jnp.float32)
    sent = [piece_of(both, place ^ m).astype(kind) for m in range(1, both.shape[0])]
    return [piece_of(both, place)], sent


def chips_received(sent):
    return [exchanged(value, "dp", 2 * (m + 1)) for m, value in enumerate(sent)]


def summed(values):
    total = values[0].astype(jnp.float32)
    for value in values[1:]:
        total = total + value.astype(jnp.float32)
    return total


def chips_gathered(value):
    return [value] + [
        exchanged(value, "dp", 2 * m) for m in range(1, lax.axis_size("dp") // 2)
    ]


def core_gathered(column):
    here = lax.axis_index("dp")
    core, place = here % 2, here // 2
    column = jnp.stack(column)
    column = jnp.stack([piece_of(column, place ^ k) for k in range(column.shape[0])])
    other = exchanged(column, "dp", 1)
    both = [jnp.where(core == 0, column, other), jnp.where(core == 0, other, column)]
    return jnp.stack(both, axis=1).reshape((-1,) + column.shape[1:])


def in_order(value, blocks):
    here = lax.axis_index("fsdp")
    pieces = jnp.stack(jnp.split(value, blocks, axis=-1))
    return jnp.concatenate([piece_of(pieces, here ^ k) for k in range(blocks)], axis=-1)


def to_workers(block, first):
    half = lax.axis_size("dp") * lax.axis_size("fsdp") // 2
    size = block.shape[2] // 2
    low, high = block[:, :, :size], block[:, :, size:]
    even = lax.ppermute(low, ("dp", "fsdp"), [(first + s, 2 * s) for s in range(half)])
    odd = lax.ppermute(high, ("dp", "fsdp"), [(first + s, 2 * s + 1) for s in range(half)])
    return even + odd


def to_owners(piece, first):
    half = lax.axis_size("dp") * lax.axis_size("fsdp") // 2
    even = lax.ppermute(piece, ("dp", "fsdp"), [(2 * s, first + s) for s in range(half)])
    odd = lax.ppermute(piece, ("dp", "fsdp"), [(2 * s + 1, first + s) for s in range(half)])
    return even, odd


def shifted(value, axis, steps):
    count = lax.axis_size(axis)
    initial, last = (max(0, -steps), min(count, count - steps))
    return lax.ppermute(value, axis, [(source, source + steps) for source in range(initial, last)])


def carried_in(decays, ends, reverse):
    count, here = lax.axis_size("fsdp"), lax.axis_index("fsdp")
    decays, ends = jnp.stack(decays), jnp.stack(ends)
    total = jnp.zeros_like(ends[0])
    for k in range(count - 1):
        at = count - 1 - k if reverse else k
        reached = at > here if reverse else at < here
        new = piece_of(decays, here ^ at) * total + piece_of(ends, here ^ at)
        total = jnp.where(reached, new, total)
    return total


def convolve(extended, conv_full, conv_shift, length):
    total = conv_shift
    for tap in range(conv_full.shape[0]):
        total = total + conv_full[tap] * extended[tap : tap + length]
    return total


def swap(value):
    return jnp.swapaxes(value, 0, 1)


def shards(
    inputs,
    modality,
    gain,
    in_weight,
    conv_weight,
    conv_bias,
    x_weight,
    dt_weight,
    dt_bias,
    log_rate,
    skip_gain,
    out_weight,
    out_grad,
):
    seq_count, length, model = inputs.shape
    copies, rank, block = in_weight.shape[0], dt_weight.shape[1], dt_weight.shape[2]
    taps, states = conv_weight.shape[0], log_rate.shape[0]
    groups, parts = lax.axis_size("dp"), lax.axis_size("fsdp")
    count = groups * seq_count
    tokens = count * length
    width = parts * block
    low, full = jnp.bfloat16, jnp.float32

    gain_row = jnp.pad(gain, (0, block - gain.shape[0]))[None]
    packed = jnp.concatenate(
        [
            gain_row,
            conv_weight,
            conv_bias[None],
            dt_bias,
            log_rate,
            skip_gain[None],
            dt_weight.reshape(copies * rank, block),
            jnp.transpose(x_weight, (0, 2, 1)).reshape(-1, block),
        ],
        axis=0,
    )
    packed = in_order(lax.all_gather(packed, "fsdp", axis=1, tiled=True), parts)
    sizes = [1, taps, 1, copies, states, 1, copies * rank, copies * (rank + 2 * states)]
    rows, at = [], 0
    for size in sizes:
        rows.append(packed[at : at + size])
        at += size
    gain_part = in_order(rows[0].reshape(parts, block)[:, : gain.shape[0]].reshape(-1), parts)
    conv_full, conv_shift = rows[1].astype(full), rows[2][0].astype(full)
    bias_step, rate_log, skip_full = rows[3].astype(full), rows[4].astype(full), rows[5][0].astype(full)
    step_full = rows[6].reshape(copies, rank, width)
    select_full = rows[7].reshape(copies, rank + 2 * states, width)

    small = jnp.concatenate([gain_part, modality.reshape(-1).astype(low)])
    small = lax.all_gather(small[None], "dp", axis=0, tiled=True)
    gain_full = small[:, : gain_part.shape[0]].reshape(model).astype(full)
    kinds = small[:, gain_part.shape[0] :].reshape(count, length)
    copy_ids = jnp.arange(copies, dtype=low)

    def masks_of(values):
        return (values.reshape(tokens)[:, None] == copy_ids[None, :]).astype(full)

    masks, masks_t = masks_of(kinds), masks_of(swap(kinds))

    x_all = lax.all_gather(inputs, "dp", axis=0, tiled=True).reshape(tokens, model)
    front_block = to_workers(in_weight, 0)
    out_parts = [out_weight] + [exchanged(out_weight, "fsdp", m) for m in range(1, parts)]
    out_parts, gate_from = then(out_parts, in_weight)
    gate_block = to_workers(gate_from, groups * parts // 2)
    x_all, g_sent = then(x_all, out_grad)
    g_all = lax.all_gather(g_sent, "dp", axis=0, tiled=True).reshape(tokens, model)
    front_full = gathered(front_block, "fsdp", 2)
    out_full = jnp.concatenate(out_parts, axis=1)

    x_float = x_all.astype(full)
    inverse = lax.rsqrt(jnp.mean(x_float * x_float, axis=-1, keepdims=True) + epsilon)
    normed = (x_float * inverse * gain_full).astype(low)

    def by_time(value):
        return swap(value.reshape(count, length, value.shape[1]))

    def by_sequence(value):
        return swap(value).reshape(tokens, value.shape[2])

    u_pre = by_time(mode_dot(normed, front_full, masks).astype(low))
    rim = in_order(shifted(in_order(u_pre[length - (taps - 1) :], parts), "fsdp", 1), parts)
    rim, gate_block = then(rim, gate_block)
    gate_parts = [gate_block] + [exchanged(gate_block, "fsdp", m) for m in range(1, parts)]
    extended = jnp.concatenate([rim, u_pre], axis=0).astype(full)
    pre_conv = convolve(extended, conv_full, conv_shift, length)
    u_act = jax.nn.silu(pre_conv)
    u_low = u_act.astype(low).reshape(tokens, width)
    proj = mode_dot_back(u_low, select_full, masks_t)
    proj, g_then = then(proj, g_all)
    kept_part, other = core_sent(proj.reshape(groups, tokens // groups, -1), full)
    d_gated = mode_dot_back(g_then, out_full, masks)
    other, d_gated = then(other, d_gated)
    own, sent = chips_sent(kept_part, other, full)
    column = chips_gathered(summed(own + chips_received(sent)))
    column, gate_parts = then(column, gate_parts)
    proj = core_gathered(column).reshape(tokens, -1)
    dt_rank = proj[:, :rank].astype(low)
    maps = proj[:, rank:]
    top = lax.reduce_precision(maps, 8, 7)
    middle = lax.reduce_precision(maps - top, 8, 7)
    thirds = jnp.concatenate([top, middle, maps - top - middle], axis=1).astype(low)
    thirds = jnp.moveaxis(thirds.reshape(length, count // SUB, SUB, 6 * states), 1, 0)
    thirds = thirds.reshape(count // SUB, length * SUB, 6 * states)
    ones = (
        jnp.arange(6 * states)[:, None] % (2 * states) == jnp.arange(2 * states * LANES)[None] // LANES
    ).astype(low)
    bias_rows = masks_t[:, 0:1] * bias_step[0]
    for copy_index in range(1, copies):
        bias_rows = bias_rows + masks_t[:, copy_index : copy_index + 1] * bias_step[copy_index]
    raw = (mode_dot(dt_rank, step_full, masks_t) + bias_rows).reshape(length, count, width)
    delta = jax.nn.softplus(raw)
    rate = -jnp.exp(rate_log)
    scaled = jnp.broadcast_to((rate * math.log2(math.e))[:, None, :], (states, SUB, width))

    def exchange_edge(edge):
        edges = [edge]
        for m in range(1, parts):
            pieces = jnp.split(exchanged(edge, "fsdp", m), parts, axis=2)
            edges.append(jnp.concatenate([pieces[q ^ m] for q in range(parts)], axis=2))
        return edges

    common = [("parts", thirds), ("ones", ones), ("rate", scaled)]
    end, total = scan_call(
        end_kernel, delta, states, False,
        [("rows", delta), ("rows", u_act)] + common, ["state", "sum"], ["spread"], 4,
    )
    edge, normed_then, gate_parts = then(
        jnp.concatenate([end, total[None]], axis=0), normed, gate_parts
    )
    edges = exchange_edge(edge)
    gate_full = jnp.concatenate(gate_parts, axis=2)
    z_low = mode_dot(normed_then, gate_full, masks).astype(low)
    edges, z_low = then(edges, z_low)
    z_gate = by_time(z_low).astype(full)
    gate = jax.nn.silu(z_gate)
    d_gated = by_time(d_gated)
    d_y = d_gated * gate
    decays = [jnp.exp(rate[:, None, :] * other[states][None]) for other in edges]
    start = carried_in(decays, [other[:states] for other in edges], False)
    (ahead,) = scan_call(
        ahead_kernel, delta, states, True,
        [("rows", delta), ("rows", d_y)] + common, ["state"], ["spread"], 4,
    )
    aheads = exchange_edge(ahead)
    y_scan, kept = scan_call(
        forward_kernel, delta, states, False,
        [("rows", delta), ("rows", u_act)] + common + [("state", start)],
        ["rows", "kept"], ["state", "spread"], 6, after=(ahead,),
    )
    y_scan, aheads = then(y_scan, aheads)
    final = carried_in(decays, aheads, True)
    mixed_out = y_scan + skip_full * u_act
    gated = by_sequence((mixed_out * gate).astype(low))
    sig_z = jax.nn.sigmoid(z_gate)
    d_z = d_gated * mixed_out * (sig_z * (1.0 + z_gate * (1.0 - sig_z)))
    d_gate = by_sequence(d_z.astype(low))

    def lowered(grad):
        return [grad[:, 0]] + [grad[:, m].astype(low) for m in range(1, parts)]

    def fsdp_received(pieces):
        return pieces[:1] + [exchanged(pieces[m], "fsdp", m) for m in range(1, parts)]

    gate_grad = lowered(mode_outer(d_gate, normed, masks).reshape(copies, parts, block, model))
    gate_grad, gated = then(gate_grad, gated)
    out_sent = mode_dot(gated, out_full, masks).astype(low).reshape(count, length, model)
    out_sent, gated = then(out_sent, gated)
    out_rows = lax.psum_scatter(out_sent, "dp", scatter_dimension=0, tiled=True)

    outer_grad = lowered(mode_outer(gated, g_all, masks).reshape(copies, parts, block, model))
    d_u_scan, d_delta, d_maps, rate_part = scan_call(
        backward_kernel, delta, states, True,
        [("rows", delta), ("rows", u_act), ("rows", d_y)] + common
        + [("kept", kept), ("state", final)],
        ["rows", "rows", "maps", "state"], ["state", "spread", "held", "factors", "spread"], 16,
        after=(out_sent, gate_grad[-1], outer_grad[-1]),
    )
    gate_received, outer_received = fsdp_received(gate_grad), fsdp_received(outer_grad)
    d_u_scan, d_delta, d_maps, rate_part, gate_received, outer_received = then(
        d_u_scan, d_delta, d_maps, rate_part, gate_received, outer_received
    )
    gate_piece = jnp.swapaxes(summed(gate_received).astype(low), 1, 2)
    out_weight_grad = summed(outer_received)
    rate_grad = rate * jnp.sum(rate_part, axis=1)
    d_raw = (d_delta * jax.nn.sigmoid(raw)).astype(low).reshape(tokens, width)
    d_rank = mode_dot_back(d_raw, step_full, masks_t)
    d_proj = jnp.concatenate([d_rank, d_maps.reshape(tokens, 2 * states)], axis=1)
    d_proj, d_gate = then(d_proj, d_gate)
    kept_part, other = core_sent(d_proj.reshape(groups, tokens // groups, -1), full)
    d_normed_gate = mode_dot_back(d_gate, gate_full, masks)
    skip_grad = jnp.sum(d_y * u_act, axis=(0, 1))
    step_grad = mode_outer(dt_rank, d_raw, masks_t)
    sbias_grad = lax.dot_general(
        masks_t.astype(low), d_raw, (((0,), (0,)), ((), ())), preferred_element_type=full
    )
    other, d_normed_gate = then(other, d_normed_gate)
    own, sent = chips_sent(kept_part, other, full)
    own = summed(own + chips_received(sent)).astype(low)
    d_proj = core_gathered(chips_gathered(own)).reshape(tokens, -1)
    d_proj, gate_piece, skip_grad, step_grad, sbias_grad, out_rows = then(
        d_proj, gate_piece, skip_grad, step_grad, sbias_grad, out_rows
    )
    output = (inputs.astype(full) + out_rows.astype(full)).astype(low)
    gate_even, gate_odd = to_owners(gate_piece, groups * parts // 2)
    d_u = (
        d_u_scan
        + skip_full * d_y
        + mode_dot(d_proj, select_full, masks_t).reshape(length, count, width)
    )
    sig_c = jax.nn.sigmoid(pre_conv)
    d_conv = d_u * (sig_c * (1.0 + pre_conv * (1.0 - sig_c)))
    rim_back = shifted(in_order(d_conv[: taps - 1].astype(low), parts), "fsdp", -1)
    d_ahead = jnp.concatenate([d_conv, in_order(rim_back, parts).astype(full)], axis=0)
    d_u_pre = convolve(d_ahead, conv_full[::-1], 0.0, length)
    d_front = by_sequence(d_u_pre.astype(low))
    d_normed = d_normed_gate + mode_dot_back(d_front, front_full, masks)
    d_sent = d_normed.astype(low).reshape(groups, seq_count, length, model)
    d_sent, d_front, gate_even, gate_odd = then(d_sent, d_front, gate_even, gate_odd)
    kept_part, other = core_sent(d_sent, low)
    gain_part = jnp.sum(d_normed * x_float * inverse, axis=0)
    gain_part, d_front = then(gain_part, d_front)
    gain_kept, gain_other = core_sent(gain_part.reshape(groups, -1), full)
    gain_own, gain_sent = chips_sent(gain_kept, gain_other, full)
    gain_part = summed(gain_own + chips_received(gain_sent))
    front_pieces = lowered(mode_outer(d_front, normed, masks).reshape(copies, parts, block, model))
    front_pieces, gain_part, d_conv, u_low = then(front_pieces, gain_part, d_conv, u_low)

    gain_rows = jnp.pad(gain_part.reshape(parts, -1), ((0, 0), (0, block - gain.shape[0])))
    select_grad = mode_outer(d_proj, u_low, masks_t)
    cshift_grad = jnp.sum(d_conv, axis=(0, 1))
    conv_grad = jnp.stack(
        [jnp.sum(d_conv * extended[tap : tap + length], axis=(0, 1)) for tap in range(taps)]
    )
    grads = jnp.concatenate(
        [
            conv_grad,
            cshift_grad[None],
            sbias_grad,
            rate_grad,
            skip_grad[None],
            step_grad.reshape(copies * rank, width),
            select_grad.reshape(-1, width),
        ],
        axis=0,
    )
    grads = jnp.concatenate([in_order(grads, parts), gain_rows.reshape(1, width)], axis=0)
    other, front_pieces, grads = then(other, front_pieces, grads)
    own, sent = chips_sent(kept_part, other, low)
    rows_received = chips_received(sent)
    front_received = fsdp_received(front_pieces)
    sent, grads = then(sent, grads)
    grads = lax.psum_scatter(grads, "fsdp", scatter_dimension=1, tiled=True)
    gain_grad = grads[-1, : gain.shape[0]]

    front_even, front_odd = to_owners(
        jnp.swapaxes(summed(front_received).astype(low), 1, 2), 0
    )
    in_weight_grad = jnp.concatenate([gate_even + front_even, gate_odd + front_odd], axis=2).astype(full)
    d_rows = summed(own + rows_received)
    own = inputs.astype(full)
    own_inverse = lax.rsqrt(jnp.mean(own * own, axis=-1, keepdims=True) + epsilon)
    d_scaled = d_rows * gain_full
    input_grad = (
        out_grad.astype(full)
        + own_inverse * d_scaled
        - own * own_inverse**3 * jnp.mean(d_scaled * own, axis=-1, keepdims=True)
    )

    rows, at = [], 0
    for size in sizes[1:]:
        rows.append(grads[at : at + size])
        at += size
    return (
        output,
        input_grad,
        gain_grad,
        in_weight_grad,
        rows[0],
        rows[1][0],
        jnp.transpose(rows[6].reshape(copies, -1, block), (0, 2, 1)),
        rows[5].reshape(copies, rank, block),
        rows[2],
        rows[3],
        rows[4][0],
        out_weight_grad,
    )


def solution(mesh):
    whole = ("dp", "fsdp")
    return jax.shard_map(
        shards,
        mesh=mesh,
        in_specs=(
            P("dp", "fsdp", None),
            P("dp", "fsdp"),
            P(whole),
            P(None, None, whole),
            P(None, whole),
            P(whole),
            P(None, whole, None),
            P(None, None, whole),
            P(None, whole),
            P(None, whole),
            P(whole),
            P(None, whole, None),
            P("dp", "fsdp", None),
        ),
        out_specs=(
            P("dp", "fsdp", None),
            P("dp", "fsdp", None),
            P(whole),
            P(None, None, whole),
            P(None, whole),
            P(whole),
            P(None, whole, None),
            P(None, None, whole),
            P(None, whole),
            P(None, whole),
            P(whole),
            P(None, whole, None),
        ),
        check_vma=False,
    )
```

```python
import functools
import math

import jax
import jax.numpy as jnp
from jax import lax
from jax.experimental import pallas as pl
from jax.experimental.pallas import tpu as pltpu
from jax.sharding import PartitionSpec as P

epsilon = 1e-05
LANES = 128
SUB = 8


def spread_maps(parts_ref, ones_ref, spread, first, last):
    chunk = spread.shape[0]
    for n in range(first, last, 2):
        both = jnp.dot(
            parts_ref[...],
            ones_ref[:, n * LANES : (n + 2) * LANES],
            preferred_element_type=jnp.float32,
        )
        spread[:, n] = both[:, :LANES].reshape(chunk, SUB, LANES)
        spread[:, n + 1] = both[:, LANES:].reshape(chunk, SUB, LANES)


def lane_blocks(width):
    return [pl.ds(start, LANES) for start in range(0, width, LANES)]


def state_blocks(states):
    return [(0, states // 2), (states // 2, states)]


def end_kernel(d_ref, u_ref, parts_ref, ones_ref, rate_ref, end_ref, sum_ref, spread):
    @pl.when(pl.program_id(1) == 0)
    def _():
        end_ref[...] = jnp.zeros_like(end_ref)
        sum_ref[...] = jnp.zeros_like(sum_ref)

    chunk, states = d_ref.shape[0], rate_ref.shape[0]
    spread_maps(parts_ref, ones_ref, spread, 0, states)
    for lanes in lane_blocks(d_ref.shape[2]):
        sum_ref[:, lanes] += jnp.sum(d_ref[:, :, lanes], axis=0)
        rate = rate_ref[:, :, lanes]

        def body(t, state):
            d, u = d_ref[t, :, lanes], u_ref[t, :, lanes]
            return jnp.exp2(d[None] * rate) * state + (d * u)[None] * spread[t, :states]

        end_ref[:, :, lanes] = lax.fori_loop(0, chunk, body, end_ref[:, :, lanes], unroll=8)


def ahead_kernel(d_ref, y_ref, parts_ref, ones_ref, rate_ref, out_ref, spread):
    @pl.when(pl.program_id(1) == 0)
    def _():
        out_ref[...] = jnp.zeros_like(out_ref)

    chunk, states = d_ref.shape[0], rate_ref.shape[0]
    spread_maps(parts_ref, ones_ref, spread, states, 2 * states)
    for lanes in lane_blocks(d_ref.shape[2]):
        rate = rate_ref[:, :, lanes]

        def body(k, grad):
            t = chunk - 1 - k
            d, dy = d_ref[t, :, lanes], y_ref[t, :, lanes]
            return jnp.exp2(d[None] * rate) * (grad + dy[None] * spread[t, states:])

        out_ref[:, :, lanes] = lax.fori_loop(0, chunk, body, out_ref[:, :, lanes], unroll=8)


def forward_kernel(
    d_ref, u_ref, parts_ref, ones_ref, rate_ref, start_ref, *refs
):
    y_ref, kept_ref, state_ref, spread = refs[-4:]

    @pl.when(pl.program_id(1) == 0)
    def _():
        state_ref[...] = start_ref[...]

    chunk, states = d_ref.shape[0], rate_ref.shape[0]
    spread_maps(parts_ref, ones_ref, spread, 0, 2 * states)
    kept_ref[0] = state_ref[...]
    for lanes in lane_blocks(d_ref.shape[2]):
        rate = rate_ref[:, :, lanes]

        def body(t, state):
            d, u = d_ref[t, :, lanes], u_ref[t, :, lanes]
            state = jnp.exp2(d[None] * rate) * state + (d * u)[None] * spread[t, :states]
            y_ref[t, :, lanes] = jnp.sum(state * spread[t, states:], axis=0)
            return state

        state_ref[:, :, lanes] = lax.fori_loop(0, chunk, body, state_ref[:, :, lanes], unroll=8)


def backward_kernel(
    d_ref,
    u_ref,
    y_ref,
    parts_ref,
    ones_ref,
    rate_ref,
    kept_ref,
    start_ref,
    *refs,
):
    du_ref, dd_ref, dmaps_ref, drate_ref, grad_ref, spread, held, factors, partial = refs[-9:]

    @pl.when(pl.program_id(1) == 0)
    def _():
        grad_ref[...] = start_ref[...]
        drate_ref[...] = jnp.zeros_like(drate_ref)

    chunk, states = d_ref.shape[0], rate_ref.shape[0]
    natural = math.log(2.0)
    spread_maps(parts_ref, ones_ref, spread, 0, 2 * states)
    for index, lanes in enumerate(lane_blocks(d_ref.shape[2])):
        for low, high in state_blocks(states):
            rate = rate_ref[low:high, :, lanes]
            held[0] = kept_ref[0, low:high, :, lanes]

            def forward(t, state):
                d, u = d_ref[t, :, lanes], u_ref[t, :, lanes]
                factor = jnp.exp2(d[None] * rate)
                state = factor * state + (d * u)[None] * spread[t, low:high]
                factors[t] = factor
                held[t + 1] = state
                return state

            lax.fori_loop(0, chunk, forward, held[0], unroll=8)

            def backward(k, carry):
                t = chunk - 1 - k
                ahead, drate = carry
                d, u, dy = d_ref[t, :, lanes], u_ref[t, :, lanes], y_ref[t, :, lanes]
                grad = spread[t, states + low : states + high] * dy[None] + ahead
                part_b = (d * u)[None] * grad
                part_c = dy[None] * held[t + 1]
                if index == 0:
                    partial[t, low:high] = part_b
                    partial[t, states + low : states + high] = part_c
                else:
                    partial[t, low:high] += part_b
                    partial[t, states + low : states + high] += part_c
                through = jnp.sum(grad * spread[t, low:high], axis=0)
                ahead = factors[t] * grad
                moved = ahead * held[t]
                du, dd = d * through, natural * jnp.sum(moved * rate, axis=0) + u * through
                if low == 0:
                    du_ref[t, :, lanes] = du
                    dd_ref[t, :, lanes] = dd
                else:
                    du_ref[t, :, lanes] += du
                    dd_ref[t, :, lanes] += dd
                return ahead, drate + d[None] * moved

            ahead, drate = lax.fori_loop(
                0,
                chunk,
                backward,
                (grad_ref[low:high, :, lanes], drate_ref[low:high, :, lanes]),
                unroll=8,
            )
            grad_ref[low:high, :, lanes] = ahead
            drate_ref[low:high, :, lanes] = drate

    column = lax.broadcasted_iota(jnp.int32, (SUB, LANES), 1)

    def gather(t, _):
        total = jnp.zeros((SUB, LANES), jnp.float32)
        for n in range(2 * states):
            total = jnp.where(column == n, jnp.sum(partial[t, n], axis=1, keepdims=True), total)
        dmaps_ref[t] = total[:, : 2 * states]
        return 0

    lax.fori_loop(0, chunk, gather, 0, unroll=8)


def scan_call(kernel, delta, states, reverse, ins, outs, scratch, cost, after=()):
    length, count, width = delta.shape
    chunk = math.gcd(16, length)
    steps = length // chunk

    def at(t):
        return steps - 1 - t if reverse else t

    specs = {
        "rows": (
            pl.BlockSpec((chunk, SUB, width), lambda b, t: (at(t), b, 0)),
            (length, count, width),
        ),
        "maps": (
            pl.BlockSpec((chunk, SUB, 2 * states), lambda b, t: (at(t), b, 0)),
            (length, count, 2 * states),
        ),
        "parts": (
            pl.BlockSpec((None, chunk * SUB, 6 * states), lambda b, t: (b, at(t), 0)),
            (count // SUB, length * SUB, 6 * states),
        ),
        "ones": (
            pl.BlockSpec((6 * states, 2 * states * LANES), lambda b, t: (0, 0)),
            (6 * states, 2 * states * LANES),
        ),
        "state": (
            pl.BlockSpec((states, SUB, width), lambda b, t: (0, b, 0)),
            (states, count, width),
        ),
        "rate": (
            pl.BlockSpec((states, SUB, width), lambda b, t: (0, 0, 0)),
            (states, SUB, width),
        ),
        "kept": (
            pl.BlockSpec((1, states, SUB, width), lambda b, t: (at(t), 0, b, 0)),
            (steps, states, count, width),
        ),
        "sum": (pl.BlockSpec((SUB, width), lambda b, t: (b, 0)), (count, width)),
    }
    sizes = {
        "spread": pltpu.VMEM((chunk, 2 * states, SUB, LANES), jnp.float32),
        "held": pltpu.VMEM((chunk + 1, states // 2, SUB, LANES), jnp.float32),
        "factors": pltpu.VMEM((chunk, states // 2, SUB, LANES), jnp.float32),
        "state": pltpu.VMEM((states, SUB, width), jnp.float32),
    }
    return pl.pallas_call(
        kernel,
        grid=(count // SUB, steps),
        in_specs=[specs[name][0] for name, _ in ins]
        + [pl.BlockSpec(memory_space=pl.ANY) for _ in after],
        out_specs=[specs[name][0] for name in outs],
        out_shape=[jax.ShapeDtypeStruct(specs[name][1], jnp.float32) for name in outs],
        scratch_shapes=[sizes[name] for name in scratch],
        compiler_params=pltpu.CompilerParams(vmem_limit_bytes=40 * 1024 * 1024),
        cost_estimate=pl.CostEstimate(
            flops=length * count * width * states * cost * 300,
            bytes_accessed=length * count * width * 4 * (len(ins) + len(outs)),
            transcendentals=length * count * width * states,
        ),
    )(*[value for _, value in ins], *after)


def masked(left, masks):
    return left[:, None, :] * masks.astype(left.dtype)[:, :, None]


def mode_dot(left, weight, masks):
    return lax.dot_general(
        masked(left, masks), weight, (((1, 2), (0, 1)), ((), ())), preferred_element_type=jnp.float32
    )


def mode_dot_back(left, weight, masks):
    return lax.dot_general(
        masked(left, masks), weight, (((1, 2), (0, 2)), ((), ())), preferred_element_type=jnp.float32
    )


def mode_outer(left, right, masks):
    return lax.dot_general(
        masked(left, masks), right, (((0,), (0,)), ((), ())), preferred_element_type=jnp.float32
    )


def outer_kernel(left_ref, right_ref, masks_ref, own_ref, *other_refs):
    block = own_ref.shape[1]
    for k in range(own_ref.shape[0]):
        total = jnp.dot(
            left_ref[...] * masks_ref[k : k + 1, :],
            right_ref[...],
            preferred_element_type=jnp.float32,
        )
        own_ref[k] = total[:block]
        for m, other_ref in enumerate(other_refs):
            other_ref[k] = total[(m + 1) * block : (m + 2) * block].astype(jnp.bfloat16)


def outer_pieces(left, right, masks, parts):
    width, tokens = left.shape
    columns, copies = right.shape[1], masks.shape[0]
    block, tile = width // parts, math.gcd(columns, 512)
    kinds = [jnp.float32] + [jnp.bfloat16] * (parts - 1)
    return pl.pallas_call(
        outer_kernel,
        grid=(columns // tile,),
        in_specs=[
            pl.BlockSpec((width, tokens), lambda n: (0, 0)),
            pl.BlockSpec((tokens, tile), lambda n: (0, n)),
            pl.BlockSpec((copies, tokens), lambda n: (0, 0)),
        ],
        out_specs=[pl.BlockSpec((copies, block, tile), lambda n: (0, 0, n))] * parts,
        out_shape=[jax.ShapeDtypeStruct((copies, block, columns), kind) for kind in kinds],
        compiler_params=pltpu.CompilerParams(vmem_limit_bytes=56 * 1024 * 1024),
        cost_estimate=pl.CostEstimate(flops=1000, bytes_accessed=1000, transcendentals=0),
    )(left, right, masks)


def back_kernel(left_ref, weight_ref, base_ref, out_ref):
    rows = math.gcd(left_ref.shape[1], 384)

    def body(i, _):
        at = pl.ds(pl.multiple_of(i * rows, rows), rows)
        total = base_ref[at, :]
        for k in range(left_ref.shape[0]):
            total = total + lax.dot_general(
                left_ref[k, at, :],
                weight_ref[k],
                (((1,), (1,)), ((), ())),
                preferred_element_type=jnp.float32,
            )
        out_ref[at, :] = total.astype(jnp.bfloat16)
        return 0

    lax.fori_loop(0, left_ref.shape[1] // rows, body, 0)


def product_back(left, weight, base):
    copies, tokens, width = left.shape
    columns = weight.shape[1]
    tile = math.gcd(columns, 512)
    return pl.pallas_call(
        back_kernel,
        grid=(columns // tile,),
        in_specs=[
            pl.BlockSpec((copies, tokens, width), lambda n: (0, 0, 0)),
            pl.BlockSpec((copies, tile, width), lambda n: (0, n, 0)),
            pl.BlockSpec((tokens, tile), lambda n: (0, n)),
        ],
        out_specs=pl.BlockSpec((tokens, tile), lambda n: (0, n)),
        out_shape=jax.ShapeDtypeStruct((tokens, columns), jnp.bfloat16),
        compiler_params=pltpu.CompilerParams(vmem_limit_bytes=56 * 1024 * 1024),
        cost_estimate=pl.CostEstimate(
            flops=2 * copies * tokens * columns * width,
            bytes_accessed=6 * tokens * columns,
            transcendentals=0,
        ),
    )(left, weight, base)


def exchanged(value, axis, mask):
    count = lax.axis_size(axis)
    return lax.ppermute(value, axis, [(source, source ^ mask) for source in range(count)])


def gathered(value, axis, dimension):
    pieces = [value] + [exchanged(value, axis, m) for m in range(1, lax.axis_size(axis))]
    return jnp.concatenate(pieces, axis=dimension)


def piece_of(pieces, index):
    return lax.dynamic_index_in_dim(pieces, index, axis=0, keepdims=False)


def then(*values):
    return lax.optimization_barrier(values)


def core_sent(pieces, kind):
    core = lax.axis_index("dp") % 2
    pairs = pieces.reshape((pieces.shape[0] // 2, 2) + pieces.shape[1:])
    kept = lax.dynamic_index_in_dim(pairs, core, axis=1, keepdims=False)
    other = lax.dynamic_index_in_dim(pairs, 1 - core, axis=1, keepdims=False)
    return kept, exchanged(other.astype(kind), "dp", 1)


def chips_sent(kept, other, kind):
    place = lax.axis_index("dp") // 2
    both = kept.astype(jnp.float32) + other.astype(jnp.float32)
    sent = [piece_of(both, place ^ m).astype(kind) for m in range(1, both.shape[0])]
    return [piece_of(both, place)], sent


def chips_received(sent):
    return [exchanged(value, "dp", 2 * (m + 1)) for m, value in enumerate(sent)]


def summed(values):
    total = values[0].astype(jnp.float32)
    for value in values[1:]:
        total = total + value.astype(jnp.float32)
    return total


def chips_gathered(value):
    return [value] + [
        exchanged(value, "dp", 2 * m) for m in range(1, lax.axis_size("dp") // 2)
    ]


def core_gathered(column):
    here = lax.axis_index("dp")
    core, place = here % 2, here // 2
    column = jnp.stack(column)
    column = jnp.stack([piece_of(column, place ^ k) for k in range(column.shape[0])])
    other = exchanged(column, "dp", 1)
    both = [jnp.where(core == 0, column, other), jnp.where(core == 0, other, column)]
    return jnp.stack(both, axis=1).reshape((-1,) + column.shape[1:])


def in_order(value, blocks):
    here = lax.axis_index("fsdp")
    pieces = jnp.stack(jnp.split(value, blocks, axis=-1))
    return jnp.concatenate([piece_of(pieces, here ^ k) for k in range(blocks)], axis=-1)


def moved(one, two, back):
    half = lax.axis_size("dp") * lax.axis_size("fsdp") // 2
    first = [(s, 2 * s) for s in range(half)] + [(half + s, 2 * s + 1) for s in range(half)]
    second = [(s, 2 * s + 1) for s in range(half)] + [(half + s, 2 * s) for s in range(half)]
    if back:
        first, second = [(b, a) for a, b in first], [(b, a) for a, b in second]
    return (
        lax.ppermute(one, ("dp", "fsdp"), first),
        lax.ppermute(two, ("dp", "fsdp"), second),
    )


def picked(choice, one, two):
    return jnp.where(choice, one, two), jnp.where(choice, two, one)


def to_workers(block):
    here = lax.axis_index(("dp", "fsdp"))
    half = lax.axis_size("dp") * lax.axis_size("fsdp") // 2
    size = block.shape[2] // 2
    sent = picked(here < half, block[:, :, :size], block[:, :, size:])
    return moved(*sent, False)


def to_owners(front, gate):
    here = lax.axis_index(("dp", "fsdp"))
    return moved(*picked(here % 2 == 0, front, gate), True)


def shifted(value, axis, steps):
    count = lax.axis_size(axis)
    initial, last = (max(0, -steps), min(count, count - steps))
    return lax.ppermute(value, axis, [(source, source + steps) for source in range(initial, last)])


def carried_in(decays, ends, reverse):
    count, here = lax.axis_size("fsdp"), lax.axis_index("fsdp")
    decays, ends = jnp.stack(decays), jnp.stack(ends)
    total = jnp.zeros_like(ends[0])
    for k in range(count - 1):
        at = count - 1 - k if reverse else k
        reached = at > here if reverse else at < here
        new = piece_of(decays, here ^ at) * total + piece_of(ends, here ^ at)
        total = jnp.where(reached, new, total)
    return total


def convolve(extended, conv_full, conv_shift, length):
    total = conv_shift
    for tap in range(conv_full.shape[0]):
        total = total + conv_full[tap] * extended[tap : tap + length]
    return total


def swap(value):
    return jnp.swapaxes(value, 0, 1)


def shards(
    inputs,
    modality,
    gain,
    in_weight,
    conv_weight,
    conv_bias,
    x_weight,
    dt_weight,
    dt_bias,
    log_rate,
    skip_gain,
    out_weight,
    out_grad,
):
    seq_count, length, model = inputs.shape
    copies, rank, block = in_weight.shape[0], dt_weight.shape[1], dt_weight.shape[2]
    taps, states = conv_weight.shape[0], log_rate.shape[0]
    groups, parts = lax.axis_size("dp"), lax.axis_size("fsdp")
    count = groups * seq_count
    tokens = count * length
    width = parts * block
    low, full = jnp.bfloat16, jnp.float32

    gain_row = jnp.pad(gain, (0, block - gain.shape[0]))[None]
    packed = jnp.concatenate(
        [
            gain_row,
            conv_weight,
            conv_bias[None],
            dt_bias,
            log_rate,
            skip_gain[None],
            dt_weight.reshape(copies * rank, block),
            jnp.transpose(x_weight, (0, 2, 1)).reshape(-1, block),
        ],
        axis=0,
    )
    packed = lax.all_gather(packed, "fsdp", axis=1, tiled=True)
    packed, out_block = then(packed, out_weight)
    packed = in_order(packed, parts)
    sizes = [1, taps, 1, copies, states, 1, copies * rank, copies * (rank + 2 * states)]
    rows, at = [], 0
    for size in sizes:
        rows.append(packed[at : at + size])
        at += size
    gain_part = in_order(rows[0].reshape(parts, block)[:, : gain.shape[0]].reshape(-1), parts)
    conv_full, conv_shift = rows[1].astype(full), rows[2][0].astype(full)
    bias_step, rate_log, skip_full = rows[3].astype(full), rows[4].astype(full), rows[5][0].astype(full)
    step_full = rows[6].reshape(copies, rank, width)
    select_full = rows[7].reshape(copies, rank + 2 * states, width)

    small = jnp.concatenate([gain_part, modality.reshape(-1).astype(low)])
    spare = -(-small.shape[0] // model)
    spare = -(-spare // 16) * 16
    small = jnp.pad(small, (0, spare * model - small.shape[0])).reshape(1, spare, model)
    x_sent = jnp.concatenate([inputs.reshape(1, seq_count * length, model), small], axis=1)
    columns = to_workers(in_weight)
    out_parts = [out_block] + [exchanged(out_block, "fsdp", m) for m in range(1, parts)]
    columns, out_parts, x_sent = then(columns, out_parts, x_sent)
    x_all = lax.all_gather(x_sent, "dp", axis=0, tiled=True)
    front_block, gate_block = picked(lax.axis_index(("dp", "fsdp")) % 2 == 0, *columns)
    front_parts = [front_block] + [exchanged(front_block, "fsdp", m) for m in range(1, parts)]
    front_parts, gate_block, g_sent = then(front_parts, gate_block, out_grad)
    front_full = jnp.concatenate(front_parts, axis=2)
    out_full = jnp.concatenate(out_parts, axis=1)
    g_all = lax.all_gather(g_sent, "dp", axis=0, tiled=True).reshape(tokens, model)
    small = x_all[:, seq_count * length :].reshape(groups, -1)
    x_all = x_all[:, : seq_count * length].reshape(tokens, model)
    gain_full = small[:, : gain_part.shape[0]].reshape(model).astype(full)
    kinds = small[:, gain_part.shape[0] : gain_part.shape[0] + seq_count * length]
    kinds = kinds.reshape(count, length)
    copy_ids = jnp.arange(copies, dtype=low)

    def masks_of(values):
        return (values.reshape(tokens)[:, None] == copy_ids[None, :]).astype(full)

    masks, masks_t = masks_of(kinds), masks_of(swap(kinds))

    x_float = x_all.astype(full)
    inverse = lax.rsqrt(jnp.mean(x_float * x_float, axis=-1, keepdims=True) + epsilon)
    normed = (x_float * inverse * gain_full).astype(low)

    def by_time(value):
        return swap(value.reshape(count, length, value.shape[1]))

    def by_sequence(value):
        return swap(value).reshape(tokens, value.shape[2])

    def by_channel(value):
        return jnp.transpose(value, (2, 1, 0)).reshape(value.shape[2], tokens)

    masks_rows = jnp.transpose(masks).astype(low)

    u_pre = by_time(mode_dot(normed, front_full, masks).astype(low))
    rim = in_order(shifted(in_order(u_pre[length - (taps - 1) :], parts), "fsdp", 1), parts)
    rim, gate_block = then(rim, gate_block)
    gate_parts = [gate_block] + [exchanged(gate_block, "fsdp", m) for m in range(1, parts)]
    extended = jnp.concatenate([rim, u_pre], axis=0).astype(full)
    pre_conv = convolve(extended, conv_full, conv_shift, length)
    u_act = jax.nn.silu(pre_conv)
    u_low = u_act.astype(low).reshape(tokens, width)
    proj = mode_dot_back(u_low, select_full, masks_t)
    proj, g_all = then(proj, g_all)
    _, normed_then = then(proj, normed)
    proj = lax.psum(proj, "dp")
    gate_full = jnp.concatenate(gate_parts, axis=2)
    z_low = mode_dot(normed_then, gate_full, masks).astype(low)
    proj, z_low = then(proj, z_low)
    z_gate = by_time(z_low).astype(full)
    gate = jax.nn.silu(z_gate)
    dt_rank = proj[:, :rank].astype(low)
    maps = proj[:, rank:]
    top = lax.reduce_precision(maps, 8, 7)
    middle = lax.reduce_precision(maps - top, 8, 7)
    thirds = jnp.concatenate([top, middle, maps - top - middle], axis=1).astype(low)
    thirds = jnp.moveaxis(thirds.reshape(length, count // SUB, SUB, 6 * states), 1, 0)
    thirds = thirds.reshape(count // SUB, length * SUB, 6 * states)
    ones = (
        jnp.arange(6 * states)[:, None] % (2 * states) == jnp.arange(2 * states * LANES)[None] // LANES
    ).astype(low)
    bias_rows = masks_t[:, 0:1] * bias_step[0]
    for copy_index in range(1, copies):
        bias_rows = bias_rows + masks_t[:, copy_index : copy_index + 1] * bias_step[copy_index]
    raw = (mode_dot(dt_rank, step_full, masks_t) + bias_rows).reshape(length, count, width)
    delta = jax.nn.softplus(raw)
    rate = -jnp.exp(rate_log)
    scaled = jnp.broadcast_to((rate * math.log2(math.e))[:, None, :], (states, SUB, width))

    def exchange_edge(edge):
        edges = [edge]
        for m in range(1, parts):
            pieces = jnp.split(exchanged(edge, "fsdp", m), parts, axis=2)
            edges.append(jnp.concatenate([pieces[q ^ m] for q in range(parts)], axis=2))
        return edges

    common = [("parts", thirds), ("ones", ones), ("rate", scaled)]
    end, total = scan_call(
        end_kernel, delta, states, False,
        [("rows", delta), ("rows", u_act)] + common, ["state", "sum"], ["spread"], 4,
    )
    edge, g_then = then(jnp.concatenate([end, total[None]], axis=0), g_all)
    edges = exchange_edge(edge)
    d_gated = mode_dot_back(g_then, out_full, masks)
    edges, d_gated = then(edges, d_gated)
    d_gated = by_time(d_gated)
    d_y = d_gated * gate
    decays = [jnp.exp(rate[:, None, :] * other[states][None]) for other in edges]
    start = carried_in(decays, [other[:states] for other in edges], False)
    (ahead,) = scan_call(
        ahead_kernel, delta, states, True,
        [("rows", delta), ("rows", d_y)] + common, ["state"], ["spread"], 4,
    )
    aheads = exchange_edge(ahead)
    y_scan, kept = scan_call(
        forward_kernel, delta, states, False,
        [("rows", delta), ("rows", u_act)] + common + [("state", start)],
        ["rows", "kept"], ["state", "spread"], 6, after=(ahead,),
    )
    y_scan, aheads = then(y_scan, aheads)
    final = carried_in(decays, aheads, True)
    mixed_out = y_scan + skip_full * u_act
    gated_low = (mixed_out * gate).astype(low)
    gated = by_sequence(gated_low)
    sig_z = jax.nn.sigmoid(z_gate)
    d_z = d_gated * mixed_out * (sig_z * (1.0 + z_gate * (1.0 - sig_z)))
    d_gate = by_sequence(d_z.astype(low))

    def fsdp_received(pieces):
        return [pieces[0]] + [exchanged(pieces[m], "fsdp", m) for m in range(1, parts)]

    gate_grad = outer_pieces(by_channel(d_z.astype(low)), normed, masks_rows, parts)
    gate_grad, gated = then(gate_grad, gated)
    out_sent = mode_dot(gated, out_full, masks).astype(low).reshape(count, length, model)
    out_sent, gated = then(out_sent, gated)
    out_rows = lax.psum_scatter(out_sent, "dp", scatter_dimension=0, tiled=True)

    _, gated_low = then(out_sent, gated_low)
    outer_grad = outer_pieces(by_channel(gated_low), g_all, masks_rows, parts)
    d_u_scan, d_delta, d_maps, rate_part = scan_call(
        backward_kernel, delta, states, True,
        [("rows", delta), ("rows", u_act), ("rows", d_y)] + common
        + [("kept", kept), ("state", final)],
        ["rows", "rows", "maps", "state"], ["state", "spread", "held", "factors", "spread"], 16,
        after=(out_sent, gate_grad[-1], outer_grad[-1]),
    )
    gate_received, outer_received = fsdp_received(gate_grad), fsdp_received(outer_grad)
    d_u_scan, d_delta, d_maps, rate_part, gate_received = then(
        d_u_scan, d_delta, d_maps, rate_part, gate_received
    )
    gate_piece = jnp.swapaxes(summed(gate_received).astype(low), 1, 2)
    rate_grad = rate * jnp.sum(rate_part, axis=1)
    d_raw = (d_delta * jax.nn.sigmoid(raw)).astype(low).reshape(tokens, width)
    d_rank = mode_dot_back(d_raw, step_full, masks_t)
    d_proj = jnp.concatenate([d_rank, d_maps.reshape(tokens, 2 * states)], axis=1)
    d_proj, d_gate, out_rows = then(d_proj, d_gate, out_rows)
    d_proj = lax.psum(d_proj, "dp")
    d_normed_gate = mode_dot_back(d_gate, gate_full, masks)
    skip_grad = jnp.sum(d_y * u_act, axis=(0, 1))
    step_grad = mode_outer(dt_rank, d_raw, masks_t)
    sbias_grad = lax.dot_general(
        masks_t.astype(low), d_raw, (((0,), (0,)), ((), ())), preferred_element_type=full
    )
    d_proj, d_normed_gate, skip_grad, step_grad, sbias_grad, outer_received = then(
        d_proj, d_normed_gate, skip_grad, step_grad, sbias_grad, outer_received
    )
    out_weight_grad = summed(outer_received)
    d_proj = lax.reduce_precision(d_proj, 8, 7).astype(low)
    output = (inputs.astype(full) + out_rows.astype(full)).astype(low)
    gate_even, gate_odd = to_owners(gate_piece, groups * parts // 2)
    d_u = (
        d_u_scan
        + skip_full * d_y
        + mode_dot(d_proj, select_full, masks_t).reshape(length, count, width)
    )
    sig_c = jax.nn.sigmoid(pre_conv)
    d_conv = d_u * (sig_c * (1.0 + pre_conv * (1.0 - sig_c)))
    rim_back = shifted(in_order(d_conv[: taps - 1].astype(low), parts), "fsdp", -1)
    d_ahead = jnp.concatenate([d_conv, in_order(rim_back, parts).astype(full)], axis=0)
    d_u_pre = convolve(d_ahead, conv_full[::-1], 0.0, length)
    d_u_low = d_u_pre.astype(low)
    d_front = by_sequence(d_u_low)
    d_front = d_front[None] * jnp.transpose(masks)[:, :, None].astype(low)
    d_sent = product_back(d_front, front_full, d_normed_gate)
    d_rows = lax.psum_scatter(
        d_sent.reshape(count, length, model), "dp", scatter_dimension=0, tiled=True
    ).astype(full)
    gain_part = jnp.sum(d_sent.astype(full) * x_float * inverse, axis=0)
    gain_part, d_u_low = then(gain_part, d_u_low)
    front_pieces = outer_pieces(by_channel(d_u_low), normed, masks_rows, parts)
    front_received = fsdp_received(front_pieces)
    _, gain_part = then(front_pieces, gain_part)
    gain_kept, gain_other = core_sent(gain_part.reshape(groups, -1), full)
    gain_own, gain_sent = chips_sent(gain_kept, gain_other, full)
    gain_part = summed(gain_own + chips_received(gain_sent))
    gain_row = jnp.pad(gain_part.reshape(parts, -1), ((0, 0), (0, block - gain.shape[0])))
    front_received, gain_row, d_conv, u_low = then(front_received, gain_row, d_conv, u_low)
    front_piece = jnp.swapaxes(summed(front_received).astype(low), 1, 2)
    returned = to_owners(front_piece, gate_piece)

    select_grad = mode_outer(d_proj, u_low, masks_t)
    cshift_grad = jnp.sum(d_conv, axis=(0, 1))
    conv_grad = jnp.stack(
        [jnp.sum(d_conv * extended[tap : tap + length], axis=(0, 1)) for tap in range(taps)]
    )
    grads = jnp.concatenate(
        [
            conv_grad,
            cshift_grad[None],
            sbias_grad,
            rate_grad,
            skip_grad[None],
            step_grad.reshape(copies * rank, width),
            select_grad.reshape(-1, width),
            in_order(gain_row.reshape(1, width), parts),
        ],
        axis=0,
    )
    grads = summed(fsdp_received([grads[:, m * block : (m + 1) * block] for m in range(parts)]))
    gain_grad = grads[-1, : gain.shape[0]]
    halves = picked(lax.axis_index(("dp", "fsdp")) < groups * parts // 2, *returned)
    in_weight_grad = jnp.concatenate(halves, axis=2).astype(full)
    own = inputs.astype(full)
    own_inverse = lax.rsqrt(jnp.mean(own * own, axis=-1, keepdims=True) + epsilon)
    d_scaled = d_rows * gain_full
    input_grad = (
        out_grad.astype(full)
        + own_inverse * d_scaled
        - own * own_inverse**3 * jnp.mean(d_scaled * own, axis=-1, keepdims=True)
    )

    rows, at = [], 0
    for size in sizes[1:]:
        rows.append(grads[at : at + size])
        at += size
    return (
        output,
        input_grad,
        gain_grad,
        in_weight_grad,
        rows[0],
        rows[1][0],
        jnp.transpose(rows[6].reshape(copies, -1, block), (0, 2, 1)),
        rows[5].reshape(copies, rank, block),
        rows[2],
        rows[3],
        rows[4][0],
        out_weight_grad,
    )


def solution(mesh):
    whole = ("dp", "fsdp")
    return jax.shard_map(
        shards,
        mesh=mesh,
        in_specs=(
            P("dp", "fsdp", None),
            P("dp", "fsdp"),
            P(whole),
            P(None, None, whole),
            P(None, whole),
            P(whole),
            P(None, whole, None),
            P(None, None, whole),
            P(None, whole),
            P(None, whole),
            P(whole),
            P(None, whole, None),
            P("dp", "fsdp", None),
        ),
        out_specs=(
            P("dp", "fsdp", None),
            P("dp", "fsdp", None),
            P(whole),
            P(None, None, whole),
            P(None, whole),
            P(whole),
            P(None, whole, None),
            P(None, None, whole),
            P(None, whole),
            P(None, whole),
            P(whole),
            P(None, whole, None),
        ),
        check_vma=False,
    )
```
